32 devices in a mesh: dp: 8 (over y, x, core), tensor: 4 (over z).
Axes of the slice: x: 2, y: 2, z: 4, core: 2. Of those that a mesh axis runs over, the one named last changes fastest.
Arguments:
- normed: bfloat16 [1024, 5376], P(('dp', 'tensor')), may hold values from -6 to 6
- grad_kv: bfloat16 [1024, 2048], P('dp', 'tensor'), may hold values from -6 to 6
- weight: bfloat16 [5376, 2048], P(None, 'tensor'), may hold values from -0.125 to 0.125
Outputs:
- grad_input: bfloat16 [1024, 5376], P(('dp', 'tensor'))
- grad_weight: float32 [5376, 2048], P('dp', 'tensor')
The draws below stay inside these ranges and needn't reach their ends.
All inputs are finite; a program needn't handle non-finite values.
Results may differ from the reference program's by a relative error of at most 0.009.
Values may be sent and summed in bfloat16 or wider, within the bound.
No kernel may reach another device: no remote copies, remote signals or barrier semaphores. Data moves between devices by JAX's collectives and lax.ppermute only.
A program may use at most 64 MiB of HBM per device.

```python
import jax
import jax.numpy as jnp
from jax import lax

FEATS = 5376
KV = 2048
TOKENS = 1024
N_TENSOR = 4


def raised(values, key, source, target, blocks, factor):
    def block_of(position):
        return (jnp.arange(values.shape[position]) // (values.shape[position] // blocks)).reshape((-1,) + (1,) * (values.ndim - 1 - position))

    one_side = jax.random.permutation(key, blocks)[block_of(target)]
    other_side = (block_of(target) + blocks // 2) % blocks
    return jnp.where((block_of(source) == one_side) | (block_of(source) == other_side), factor * values, values)


def block_scale(own_key, shape, split, smallest, top_value):
    def one(position, blocks):
        heights = jax.random.uniform(jax.random.fold_in(jax.random.fold_in(own_key, 6), position), (blocks,), jnp.float32, smallest / len(split), top_value / len(split))
        return jnp.repeat(jnp.exp(heights), shape[position] // blocks).reshape((-1,) + (1,) * (len(shape) - position - 1))

    level = one(*split[0])
    for cut in split[1:]:
        level = level * one(*cut)
    return level


def normal_values(own_key, shape, spread, limit, cuts=(), kind=jnp.bfloat16):
    factor_of = block_scale(own_key, shape, cuts, -0.22, 0.18) if cuts else 1.0
    array = jax.random.normal(own_key, shape, jnp.float32) * spread * factor_of
    return jnp.minimum(jnp.maximum(array, -limit), limit).astype(kind)


def heavy_noise(stream_key, dims, deviation, reach, split, heavy, kind=jnp.bfloat16):
    result = deviation * jax.random.normal(stream_key, dims, jnp.float32)
    if split:
        result = result * block_scale(stream_key, dims, split, -0.22, 0.18)
    return jnp.clip(raised(result, jax.random.fold_in(stream_key, 3), *heavy), -reach, reach).astype(kind)


def setup_inputs(seed: int = 0) -> dict:
    splits = jax.random.split(jax.random.key(seed), 4)
    return {
        "normed": heavy_noise(splits[0], (TOKENS, FEATS), 1.0, 6.0, ((0, 32),), (0, 1, 32, 2.75)),
        "grad_kv": normal_values(splits[1], (TOKENS, KV), 1.0, 6.0, ((0, 8), (1, 4))),
        "weight": normal_values(splits[2], (FEATS, KV), KV ** -0.5, 0.125, ((1, 4),)),
    }


def reference(normed, grad_kv, weight):
    width = KV // N_TENSOR

    def add_block(total, index):
        begin = (index * width).astype(jnp.int32)
        cotangent = lax.dynamic_slice_in_dim(grad_kv, begin, width, 1)
        columns = lax.dynamic_slice_in_dim(weight, begin, width, 1)
        term = lax.dot_general(cotangent, columns, (((1,), (1,)), ((), ())), preferred_element_type=jnp.float32)
        term = lax.optimization_barrier(term.astype(jnp.bfloat16))
        return total + term.astype(jnp.float32), None

    initial = jnp.zeros((TOKENS, FEATS), jnp.float32)
    summed, unused = lax.scan(add_block, initial, jnp.arange(N_TENSOR, dtype=jnp.int32))
    grad_weight = lax.dot_general(normed, grad_kv, (((0,), (0,)), ((), ())), preferred_element_type=jnp.float32)
    return summed.astype(jnp.bfloat16), grad_weight
```

```python
import functools
import math

import jax
import jax.numpy as jnp
from jax import lax
from jax.experimental import pallas as pl
from jax.experimental.pallas import tpu as pltpu
from jax.sharding import PartitionSpec as P

BF16 = jnp.bfloat16
F32 = jnp.float32
LANES = 128
VMEM = pl.BlockSpec(memory_space=pltpu.VMEM)
PARAMS = pltpu.CompilerParams(vmem_limit_bytes=48 * 1024 * 1024)


class Plan:
    def __init__(self, mesh, normed, grad_kv):
        self.n_dp, self.n_t = mesh.shape["dp"], mesh.shape["tensor"]
        self.chips = self.n_dp // 2
        self.rows, self.feats = normed.shape
        self.kv = grad_kv.shape[1]
        self.width = self.feats // self.n_dp
        self.tokens = self.rows * self.n_dp
        self.tiles = self.feats // LANES
        starts = [self.width * d // LANES * LANES for d in range(self.n_dp)]
        ends = [self.width * d - s + self.width for d, s in enumerate(starts)]
        self.window = -(-max(ends) // LANES) * LANES
        self.step = math.gcd(self.width, LANES)
        self.power = self.chips & (self.chips - 1) == 0

    def chip_to(self, chip, q):
        return chip ^ q if self.power else lax.rem(chip + q, self.chips) if not isinstance(chip, int) else (chip + q) % self.chips

    def chip_from(self, chip, q):
        return chip ^ q if self.power else lax.rem(chip + self.chips - q, self.chips)

    def start_of(self, d):
        exact = d * self.width
        return jnp.minimum(exact // LANES * LANES, self.feats - self.window)

    def swap_cores(self, x):
        return lax.ppermute(x, "dp", [(d, d ^ 1) for d in range(self.n_dp)])

    def to_chip(self, x, q):
        return lax.ppermute(x, "dp", [(d, 2 * self.chip_to(d // 2, q) + d % 2) for d in range(self.n_dp)])

    def along(self, x):
        pairs = []
        for d in range(self.n_dp):
            for t in range(self.n_t):
                to = t - 1 if d % 2 else t + 1
                pairs.append((d * self.n_t + t, d * self.n_t + to if 0 <= to < self.n_t else (d ^ 1) * self.n_t + t))
        return lax.ppermute(x, ("dp", "tensor"), pairs)


def split_kernel(plan, normed_ref, keep_ref, send_ref):
    d = lax.axis_index("dp")
    chip, core = d // 2, d % 2
    for q in range(plan.chips):
        to = plan.chip_to(chip, q)
        for ref, c in ((keep_ref, core), (send_ref, 1 - core)):
            start = pl.multiple_of(plan.start_of(2 * to + c), LANES)
            ref[q] = normed_ref[:, pl.ds(start, plan.window)]


def turn_kernel(plan, *refs):
    *pieces, out_ref, scratch = refs
    d = lax.axis_index("dp")
    offset = pl.multiple_of(d * plan.width - plan.start_of(d), plan.step)
    per_tile = LANES // pieces[0].shape[0]
    for j in range(plan.tokens // LANES):
        tile = jnp.concatenate([ref[...] for ref in pieces[j * per_tile : (j + 1) * per_tile]], axis=0)
        scratch[...] = tile.T
        out_ref[j] = scratch[pl.ds(offset, plan.width), :]


def partial_kernel(plan, own_ref, other_ref, weight_ref, out_ref):
    both = jnp.concatenate([own_ref[...], other_ref[...]], axis=0)
    product = lax.dot_general(both, weight_ref[...], (((1,), (1,)), ((), ())), preferred_element_type=F32).astype(BF16)
    for r in range(out_ref.shape[0]):
        for j in range(out_ref.shape[1]):
            out_ref[r, j] = product[r * plan.rows : (r + 1) * plan.rows, j * LANES : (j + 1) * LANES]


def weight_kernel(plan, *refs):
    n = plan.n_t
    kv_ref, own_ref, *blocks, out_ref = refs
    mine, theirs = blocks[: n - 1], blocks[n - 1 :]
    d, t = lax.axis_index("dp"), lax.axis_index("tensor")
    chip, core = d // 2, d % 2
    place = jnp.where(core == 0, t, n - 1 - t)
    for k in range(n):
        source = jnp.where(core == 0, lax.rem(t + n - k, n), lax.rem(t + k, n))
        rows = []
        for q in range(plan.chips):
            at = 2 * plan.chip_from(chip, q)
            rows += [kv_ref[at + core, source], kv_ref[at + 1 - core, source]]
        rows = jnp.concatenate(rows, axis=0)
        if k:
            block = jnp.where(place >= k, mine[k - 1][...], theirs[n - k - 1][...])
        else:
            block = own_ref[...]
        block = block.reshape(plan.tokens // LANES, plan.width, LANES)
        block = jnp.concatenate([block[j] for j in range(plan.tokens // LANES)], axis=1)
        term = jnp.dot(block, rows, preferred_element_type=F32)
        if k:
            out_ref[...] += term
        else:
            out_ref[...] = term


def input_kernel(plan, partial_ref, mine_ref, theirs_ref, out_ref):
    n = plan.n_t
    core, t = lax.axis_index("dp") % 2, lax.axis_index("tensor")
    place = jnp.where(core == 0, t, n - 1 - t)
    for j in range(plan.tiles):
        total = partial_ref[t, j].astype(F32)
        total += jnp.where(place >= 1, mine_ref[j].astype(F32), 0.0)
        total += jnp.where(place < n - 1, theirs_ref[j].astype(F32), 0.0)
        out_ref[:, j * LANES : (j + 1) * LANES] = total.astype(BF16)


def body(mesh, normed, grad_kv, weight):
    plan = Plan(mesh, normed, grad_kv)
    n = plan.n_t
    flat = (plan.tiles, plan.rows, LANES)
    d, t = lax.axis_index("dp"), lax.axis_index("tensor")
    core = d % 2
    place = jnp.where(core == 0, t, n - 1 - t)

    all_kv = lax.all_gather(grad_kv, "dp", axis=0, tiled=False)
    other_kv = plan.swap_cores(grad_kv)

    pieces = jax.ShapeDtypeStruct((plan.chips, plan.rows, plan.window), BF16)
    keep, send = pl.pallas_call(
        functools.partial(split_kernel, plan), out_shape=(pieces, pieces), in_specs=[VMEM], out_specs=(VMEM, VMEM),
        compiler_params=PARAMS, name="split",
    )(normed)
    got = plan.swap_cores(send)
    pairs = [jnp.concatenate([keep[q], got[q]], axis=0) for q in range(plan.chips)]
    pairs = [plan.to_chip(pairs[q], q) if q else pairs[q] for q in range(plan.chips)]

    targets = 2 * n
    group = 6
    part = pl.pallas_call(
        functools.partial(partial_kernel, plan),
        out_shape=jax.ShapeDtypeStruct((targets,) + flat, BF16),
        grid=(plan.tiles // group,),
        in_specs=[
            pl.BlockSpec(grad_kv.shape, lambda i: (0, 0)),
            pl.BlockSpec(grad_kv.shape, lambda i: (0, 0)),
            pl.BlockSpec((group * LANES, plan.kv), lambda i: (i, 0)),
        ],
        out_specs=pl.BlockSpec((targets, group, plan.rows, LANES), lambda i: (0, i, 0, 0)),
        compiler_params=PARAMS, name="partials",
        cost_estimate=pl.CostEstimate(flops=4 * grad_kv.size * plan.feats, bytes_accessed=weight.size * 2 + targets * normed.size * 2, transcendentals=0),
    )(grad_kv, other_kv, weight)
    part_own, part_other = part[:n], part[n:]

    own = pl.pallas_call(
        functools.partial(turn_kernel, plan),
        out_shape=jax.ShapeDtypeStruct((plan.tokens // LANES, plan.width, LANES), BF16),
        in_specs=[VMEM] * plan.chips, out_specs=VMEM,
        scratch_shapes=[pltpu.VMEM((plan.window, LANES), BF16)],
        compiler_params=PARAMS, name="turn",
    )(*pairs).reshape(flat)
    other = plan.swap_cores(own)

    def passed(received, partial, slot):
        target = jnp.clip(jnp.where(core == 0, t + n - slot + 1, t - (n - slot + 1)), 0, n - 1)
        mine = lax.dynamic_index_in_dim(partial, target, 0, keepdims=False).astype(F32)
        arrived = jnp.where(place >= 1, received.astype(F32), 0.0)
        return (arrived + jnp.where(place < slot - 1, mine, 0.0)).astype(BF16)

    mine, theirs = [], []
    first, second = plan.along(own), plan.along(other)
    for slot in range(2, n + 1):
        mine.append(first)
        theirs.append(plan.swap_cores(second))
        first, second = plan.along(passed(first, part_other, slot)), plan.along(passed(second, part_own, slot))
    rest = plan.swap_cores(first)

    grad_weight = pl.pallas_call(
        functools.partial(weight_kernel, plan),
        out_shape=jax.ShapeDtypeStruct((plan.width, plan.kv), F32),
        in_specs=[VMEM] * (2 * n), out_specs=VMEM,
        compiler_params=PARAMS, name="weights",
        cost_estimate=pl.CostEstimate(flops=2 * n * normed.size * plan.kv, bytes_accessed=4 * plan.width * plan.kv, transcendentals=0),
    )(all_kv.reshape(plan.n_dp, n, plan.rows, plan.kv), own, *mine, *theirs)

    grad_input = pl.pallas_call(
        functools.partial(input_kernel, plan),
        out_shape=jax.ShapeDtypeStruct(normed.shape, BF16),
        in_specs=[VMEM] * 3, out_specs=VMEM,
        compiler_params=PARAMS, name="inputs",
    )(part_own, second, rest)
    return grad_input, grad_weight


def solution(mesh):
    in_specs = (P(("dp", "tensor"), None), P("dp", "tensor"), P(None, "tensor"))
    out_specs = (P(("dp", "tensor"), None), P("dp", "tensor"))
    return jax.shard_map(functools.partial(body, mesh), mesh=mesh, in_specs=in_specs, out_specs=out_specs, check_vma=False)
```

```python
import functools
import math

import jax
import jax.numpy as jnp
from jax import lax
from jax.experimental import pallas as pl
from jax.experimental.pallas import tpu as pltpu
from jax.sharding import PartitionSpec as P

LIMIT = 8
TWICE = 0
SPLIT = 1
COST = 1 * 10**8
BF16 = jnp.bfloat16
F32 = jnp.float32
LANES = 128
VMEM = pl.BlockSpec(memory_space=pltpu.VMEM)
ANY = pl.BlockSpec(memory_space=pl.ANY)
PARAMS = pltpu.CompilerParams(vmem_limit_bytes=LIMIT * 1024 * 1024)


class Plan:
    def __init__(self, mesh, normed, grad_kv):
        self.n_dp, self.n_t = mesh.shape["dp"], mesh.shape["tensor"]
        self.chips = self.n_dp // 2
        self.rows, self.feats = normed.shape
        self.kv = grad_kv.shape[1]
        self.width = self.feats // self.n_dp
        self.tokens = self.rows * self.n_dp
        self.tiles = self.feats // LANES
        self.half_tiles = self.tokens // 2 // LANES
        starts = [self.width * d // LANES * LANES for d in range(self.n_dp)]
        ends = [self.width * d - s + self.width for d, s in enumerate(starts)]
        self.window = -(-max(ends) // LANES) * LANES
        self.step = math.gcd(self.width, LANES)
        self.power = self.chips & (self.chips - 1) == 0

    def chip_to(self, chip, q):
        return chip ^ q if self.power else lax.rem(chip + q, self.chips) if not isinstance(chip, int) else (chip + q) % self.chips

    def chip_from(self, chip, q):
        return chip ^ q if self.power else lax.rem(chip + self.chips - q, self.chips)

    def start_of(self, d):
        exact = d * self.width
        return jnp.minimum(exact // LANES * LANES, self.feats - self.window)

    def swap_cores(self, x):
        return lax.ppermute(x, "dp", [(d, d ^ 1) for d in range(self.n_dp)])

    def to_chip(self, x, q):
        return lax.ppermute(x, "dp", [(d, 2 * self.chip_to(d // 2, q) + d % 2) for d in range(self.n_dp)])

    def along(self, x):
        pairs = []
        for d in range(self.n_dp):
            for t in range(self.n_t):
                to = t - 1 if d % 2 else t + 1
                pairs.append((d * self.n_t + t, d * self.n_t + to if 0 <= to < self.n_t else (d ^ 1) * self.n_t + t))
        return lax.ppermute(x, ("dp", "tensor"), pairs)


def split_kernel(plan, normed_ref, *out_refs):
    chip = lax.axis_index("dp") // 2
    for q, out_ref in enumerate(out_refs):
        for group in range(2):
            start = pl.multiple_of(plan.start_of(2 * plan.chip_to(chip, q) + group), LANES)
            out_ref[group] = normed_ref[:, pl.ds(start, plan.window)]


def turn_kernel(plan, *refs):
    pieces, out_ref, scratch = refs[: plan.chips], refs[-2], refs[-1]
    chip = lax.axis_index("dp") // 2
    per_tile = LANES // plan.rows
    for group in range(2):
        d = 2 * chip + group
        offset = pl.multiple_of(d * plan.width - plan.start_of(d), plan.step)
        for j in range(plan.half_tiles):
            tile = jnp.concatenate([ref[group] for ref in pieces[j * per_tile : (j + 1) * per_tile]], axis=0)
            scratch[...] = tile.T
            out_ref[group, j] = scratch[pl.ds(offset, plan.width), :]


def partial_kernel(plan, own_ref, other_ref, *refs):
    weights, out_refs = refs[:-2], refs[-2:]
    both = jnp.concatenate([own_ref[...], other_ref[...]], axis=0)
    product = lax.dot_general(both, jnp.concatenate([ref[...] for ref in weights], axis=0), (((1,), (1,)), ((), ())), preferred_element_type=F32).astype(BF16)
    for half, out_ref in enumerate(out_refs):
        for r in range(plan.n_t):
            at = (half * plan.n_t + r) * plan.rows
            for j in range(out_ref.shape[1]):
                out_ref[r, j] = product[at : at + plan.rows, j * LANES : (j + 1) * LANES]


def pass_kernel(plan, slot, received_ref, partial_ref, *refs):
    n, out_ref = plan.n_t, refs[-1]
    core, t = lax.axis_index("dp") % 2, lax.axis_index("tensor")
    place = jnp.where(core == 0, t, n - 1 - t)
    target = jnp.clip(jnp.where(core == 0, t + n - slot + 1, t - (n - slot + 1)), 0, n - 1)

    @pl.when(place >= slot - 1)
    def _():
        out_ref[...] = received_ref[...]

    @pl.when(place == 0)
    def _():
        out_ref[...] = partial_ref[target]

    @pl.when((place > 0) & (place < slot - 1))
    def _():
        for j in range(plan.tiles):
            out_ref[j] = (received_ref[j].astype(F32) + partial_ref[target, j].astype(F32)).astype(BF16)


def weight_kernel(plan, *refs):
    n, half = plan.n_t, plan.tokens // 2 // plan.n_t
    kv_refs, own, theirs = refs[:2], refs[2 : 2 + 2 * n], refs[2 + 2 * n : -4]
    out_ref, token_ref, block, rows = refs[-4:]
    core, t = lax.axis_index("dp") % 2, lax.axis_index("tensor")
    place = jnp.where(core == 0, t, n - 1 - t)
    shape = (plan.half_tiles, plan.width, LANES)
    for k in range(n):
        source = jnp.where(core == 0, lax.rem(t + n - k, n), lax.rem(t + k, n))
        at = pl.ds(pl.multiple_of(source * plan.rows, plan.rows), plan.rows)
        for parity in range(2):
            begin = (2 * k + parity) * plan.half_tiles * LANES
            for q in range(plan.chips):
                rows[begin + q * plan.rows : begin + (q + 1) * plan.rows, :] = kv_refs[parity][q, at, :]

            def fill(ref, group):
                piece = ref[group].reshape(shape)
                for j in range(plan.half_tiles):
                    block[:, begin + j * LANES : begin + (j + 1) * LANES] = piece[j]

            if k:
                pl.when(place >= k)(lambda: fill(own[2 * k + parity], core))
                pl.when(place < k)(lambda: fill(theirs[n - k - 1], 1 - parity))
            else:
                fill(own[parity], core)
    token_ref[...] = jnp.zeros_like(token_ref)
    out_ref[...] = jnp.dot(block[...], rows[...], preferred_element_type=F32)


def pick_kernel(first_ref, second_ref, out_ref):
    core = lax.axis_index("dp") % 2
    out_ref[0] = first_ref[1 - core]
    out_ref[1] = second_ref[1 - core]


def stack_kernel(*refs):
    for i, ref in enumerate(refs[:-1]):
        refs[-1][i] = ref[...]


def hold_kernel(x_ref, after_ref, out_ref):
    out_ref[...] = x_ref[...]


def half_kernel(plan, partial_ref, mine_ref, after_ref, out_ref):
    n = plan.n_t
    core, t = lax.axis_index("dp") % 2, lax.axis_index("tensor")
    place = jnp.where(core == 0, t, n - 1 - t)
    for j in range(plan.tiles):
        out_ref[j] = partial_ref[t, j].astype(F32) + jnp.where(place >= 1, mine_ref[j].astype(F32), 0.0)


def input_kernel(plan, half_ref, theirs_ref, out_ref):
    n = plan.n_t
    core, t = lax.axis_index("dp") % 2, lax.axis_index("tensor")
    place = jnp.where(core == 0, t, n - 1 - t)
    for j in range(plan.tiles):
        total = half_ref[j] + jnp.where(place < n - 1, theirs_ref[j].astype(F32), 0.0)
        out_ref[:, j * LANES : (j + 1) * LANES] = total.astype(BF16)


def body(mesh, normed, grad_kv, weight):
    plan = Plan(mesh, normed, grad_kv)
    n = plan.n_t
    flat = (plan.tiles, plan.rows, LANES)
    halves = (2, plan.tiles // 2, plan.rows, LANES)
    core = lax.axis_index("dp") % 2

    other_kv = plan.swap_cores(grad_kv)
    near_kv = plan.swap_cores(other_kv) if TWICE else grad_kv
    pieces = pl.pallas_call(
        functools.partial(split_kernel, plan),
        out_shape=[jax.ShapeDtypeStruct((2, plan.rows, plan.window), BF16)] * plan.chips,
        in_specs=[VMEM], out_specs=[VMEM] * plan.chips, compiler_params=PARAMS, name="split",
    )(normed)
    order = range(plan.chips - 1, 0, -1)
    moved = {q: plan.to_chip(pieces[q], q) for q in order}
    pieces = [pieces[0]] + [moved[q] for q in range(1, plan.chips)]

    group = 6
    part_own, part_other = pl.pallas_call(
        functools.partial(partial_kernel, plan),
        out_shape=[jax.ShapeDtypeStruct((n,) + flat, BF16)] * 2,
        grid=(plan.tiles // group,),
        in_specs=[
            pl.BlockSpec(grad_kv.shape, lambda i: (0, 0)),
            pl.BlockSpec(grad_kv.shape, lambda i: (0, 0)),
        ]
        + [pl.BlockSpec((group * LANES // SPLIT, plan.kv), functools.partial(lambda j, i: (SPLIT * i + j, 0), j)) for j in range(SPLIT)],
        out_specs=[pl.BlockSpec((n, group, plan.rows, LANES), lambda i: (0, i, 0, 0))] * 2,
        compiler_params=PARAMS, name="partials",
        cost_estimate=pl.CostEstimate(flops=4 * grad_kv.size * plan.feats, bytes_accessed=weight.size * 2 + 2 * n * normed.size * 2, transcendentals=0),
    )(near_kv, other_kv, *[weight] * SPLIT)

    first = pl.pallas_call(
        functools.partial(turn_kernel, plan),
        out_shape=jax.ShapeDtypeStruct((2, plan.half_tiles, plan.width, LANES), BF16),
        in_specs=[VMEM] * plan.chips + [ANY], out_specs=VMEM,
        scratch_shapes=[pltpu.VMEM((plan.window, LANES), BF16)],
        compiler_params=PARAMS, name="turn",
    )(*pieces, part_own).reshape(flat)
    second = plan.swap_cores(first)

    def passed(received, partial, slot, after):
        return pl.pallas_call(
            functools.partial(pass_kernel, plan, slot),
            out_shape=jax.ShapeDtypeStruct(flat, BF16),
            in_specs=[VMEM] * 2 + [ANY] * len(after), out_specs=VMEM, compiler_params=PARAMS, name="passed",
            cost_estimate=pl.CostEstimate(flops=COST, bytes_accessed=0, transcendentals=0),
        )(received, partial, *after)

    own, theirs = [first.reshape(halves), second.reshape(halves)], []
    first, second = plan.along(first), plan.along(second)

    held_kv = pl.pallas_call(
        hold_kernel, out_shape=jax.ShapeDtypeStruct(grad_kv.shape, BF16),
        in_specs=[VMEM, ANY], out_specs=VMEM, compiler_params=PARAMS, name="hold",
    )(near_kv, first)
    kv = pl.pallas_call(
        stack_kernel, out_shape=jax.ShapeDtypeStruct((plan.chips,) + grad_kv.shape, BF16),
        in_specs=[VMEM] * plan.chips, out_specs=VMEM, compiler_params=PARAMS, name="stack",
    )(*[plan.to_chip(held_kv, q) if q else held_kv for q in range(plan.chips)])
    kvs = [kv, plan.swap_cores(kv)]
    trail = [own[1], second]
    for slot in range(2, n + 1):
        got = [first.reshape(halves), second.reshape(halves)]
        own += got
        sent = [passed(first, part_other, slot, [trail[slot - 2]]), passed(second, part_own, slot, theirs[-1:])]
        first, second = plan.along(sent[0]), plan.along(sent[1])
        trail.append(second)
        theirs.append(plan.swap_cores(pl.pallas_call(
            pick_kernel, out_shape=jax.ShapeDtypeStruct(halves, BF16), in_specs=[VMEM] * 2, out_specs=VMEM,
            compiler_params=PARAMS, name="pick",
        )(*got)))
    rest = plan.swap_cores(first)

    grad_weight, token = pl.pallas_call(
        functools.partial(weight_kernel, plan),
        out_shape=(jax.ShapeDtypeStruct((plan.width, plan.kv), F32), jax.ShapeDtypeStruct((8, LANES), F32)),
        in_specs=[VMEM] * (3 * n + 1), out_specs=(VMEM, VMEM),
        scratch_shapes=[pltpu.VMEM((plan.width, n * plan.tokens), BF16), pltpu.VMEM((n * plan.tokens, plan.kv), BF16)],
        compiler_params=pltpu.CompilerParams(vmem_limit_bytes=8 * 1024 * 1024 + 4 * n * plan.tokens * (plan.width + plan.kv)), name="weights",
        cost_estimate=pl.CostEstimate(flops=2 * n * normed.size * plan.kv, bytes_accessed=4 * plan.width * plan.kv, transcendentals=0),
    )(*kvs, *own, *theirs)

    half = pl.pallas_call(
        functools.partial(half_kernel, plan),
        out_shape=jax.ShapeDtypeStruct(flat, F32),
        in_specs=[VMEM] * 2 + [ANY], out_specs=VMEM,
        compiler_params=PARAMS, name="half",
        cost_estimate=pl.CostEstimate(flops=COST, bytes_accessed=0, transcendentals=0),
    )(part_own, second, token)
    grad_input = pl.pallas_call(
        functools.partial(input_kernel, plan),
        out_shape=jax.ShapeDtypeStruct(normed.shape, BF16),
        in_specs=[VMEM] * 2, out_specs=VMEM,
        compiler_params=PARAMS, name="inputs",
    )(half, rest)
    return grad_input, grad_weight


def solution(mesh):
    in_specs = (P(("dp", "tensor"), None), P("dp", "tensor"), P(None, "tensor"))
    out_specs = (P(("dp", "tensor"), None), P("dp", "tensor"))
    return jax.shard_map(functools.partial(body, mesh), mesh=mesh, in_specs=in_specs, out_specs=out_specs, check_vma=False)
```

```python
import functools
import math

import jax
import jax.numpy as jnp
from jax import lax
from jax.experimental import pallas as pl
from jax.experimental.pallas import tpu as pltpu
from jax.sharding import PartitionSpec as P

LIMIT = 8
TWICE = 0
SPLIT = 1
COST = 10**6
BF16 = jnp.bfloat16
F32 = jnp.float32
LANES = 128
VMEM = pl.BlockSpec(memory_space=pltpu.VMEM)
ANY = pl.BlockSpec(memory_space=pl.ANY)
PARAMS = pltpu.CompilerParams(vmem_limit_bytes=LIMIT * 1024 * 1024)


class Plan:
    def __init__(self, mesh, normed, grad_kv):
        self.n_dp, self.n_t = mesh.shape["dp"], mesh.shape["tensor"]
        self.chips = self.n_dp // 2
        self.rows, self.feats = normed.shape
        self.kv = grad_kv.shape[1]
        self.width = self.feats // self.n_dp
        self.tokens = self.rows * self.n_dp
        self.tiles = self.feats // LANES
        self.half_tiles = self.tokens // 2 // LANES
        starts = [self.width * d // LANES * LANES for d in range(self.n_dp)]
        ends = [self.width * d - s + self.width for d, s in enumerate(starts)]
        self.window = -(-max(ends) // LANES) * LANES
        self.step = math.gcd(self.width, LANES)
        self.power = self.chips & (self.chips - 1) == 0

    def chip_to(self, chip, q):
        return chip ^ q if self.power else lax.rem(chip + q, self.chips) if not isinstance(chip, int) else (chip + q) % self.chips

    def chip_from(self, chip, q):
        return chip ^ q if self.power else lax.rem(chip + self.chips - q, self.chips)

    def start_of(self, d):
        exact = d * self.width
        return jnp.minimum(exact // LANES * LANES, self.feats - self.window)

    def swap_cores(self, x):
        return lax.ppermute(x, "dp", [(d, d ^ 1) for d in range(self.n_dp)])

    def to_chip(self, x, q):
        return lax.ppermute(x, "dp", [(d, 2 * self.chip_to(d // 2, q) + d % 2) for d in range(self.n_dp)])

    def along(self, x):
        pairs = []
        for d in range(self.n_dp):
            for t in range(self.n_t):
                to = t - 1 if d % 2 else t + 1
                pairs.append((d * self.n_t + t, d * self.n_t + to if 0 <= to < self.n_t else (d ^ 1) * self.n_t + t))
        return lax.ppermute(x, ("dp", "tensor"), pairs)


def split_kernel(plan, normed_ref, *out_refs):
    chip = lax.axis_index("dp") // 2
    for q, out_ref in enumerate(out_refs):
        for group in range(2):
            start = pl.multiple_of(plan.start_of(2 * plan.chip_to(chip, q) + group), LANES)
            out_ref[group] = normed_ref[:, pl.ds(start, plan.window)]


def turn_kernel(plan, *refs):
    pieces, out_ref, scratch = refs[: plan.chips], refs[-2], refs[-1]
    chip = lax.axis_index("dp") // 2
    per_tile = LANES // plan.rows
    for group in range(2):
        d = 2 * chip + group
        offset = pl.multiple_of(d * plan.width - plan.start_of(d), plan.step)
        for j in range(plan.half_tiles):
            tile = jnp.concatenate([ref[group] for ref in pieces[j * per_tile : (j + 1) * per_tile]], axis=0)
            scratch[...] = tile.T
            out_ref[group, j] = scratch[pl.ds(offset, plan.width), :]


def partial_kernel(plan, own_ref, other_ref, *refs):
    weights, out_refs = refs[:-2], refs[-2:]
    both = jnp.concatenate([own_ref[...], other_ref[...]], axis=0)
    product = lax.dot_general(both, jnp.concatenate([ref[...] for ref in weights], axis=0), (((1,), (1,)), ((), ())), preferred_element_type=F32).astype(BF16)
    for half, out_ref in enumerate(out_refs):
        for r in range(plan.n_t):
            at = (half * plan.n_t + r) * plan.rows
            for j in range(out_ref.shape[1]):
                out_ref[r, j] = product[at : at + plan.rows, j * LANES : (j + 1) * LANES]


def pass_kernel(plan, slot, received_ref, partial_ref, *refs):
    n, out_ref = plan.n_t, refs[-1]
    core, t = lax.axis_index("dp") % 2, lax.axis_index("tensor")
    place = jnp.where(core == 0, t, n - 1 - t)
    target = jnp.clip(jnp.where(core == 0, t + n - slot + 1, t - (n - slot + 1)), 0, n - 1)

    @pl.when(place >= slot - 1)
    def _():
        out_ref[...] = received_ref[...]

    @pl.when(place == 0)
    def _():
        out_ref[...] = partial_ref[target]

    @pl.when((place > 0) & (place < slot - 1))
    def _():
        for j in range(plan.tiles):
            out_ref[j] = (received_ref[j].astype(F32) + partial_ref[target, j].astype(F32)).astype(BF16)


def weight_kernel(plan, *refs):
    n, half = plan.n_t, plan.tokens // 2 // plan.n_t
    kv_refs, own, theirs = refs[:2], refs[2 : 2 + 2 * n], refs[2 + 2 * n : -4]
    out_ref, token_ref, block, rows = refs[-4:]
    core, t = lax.axis_index("dp") % 2, lax.axis_index("tensor")
    place = jnp.where(core == 0, t, n - 1 - t)
    shape = (plan.half_tiles, plan.width, LANES)
    for k in range(n):
        source = jnp.where(core == 0, lax.rem(t + n - k, n), lax.rem(t + k, n))
        at = pl.ds(pl.multiple_of(source * plan.rows, plan.rows), plan.rows)
        for parity in range(2):
            begin = (2 * k + parity) * plan.half_tiles * LANES
            for q in range(plan.chips):
                rows[begin + q * plan.rows : begin + (q + 1) * plan.rows, :] = kv_refs[parity][q, at, :]

            def fill(ref, group):
                piece = ref[group].reshape(shape)
                for j in range(plan.half_tiles):
                    block[:, begin + j * LANES : begin + (j + 1) * LANES] = piece[j]

            if k:
                pl.when(place >= k)(lambda: fill(own[2 * k + parity], core))
                pl.when(place < k)(lambda: fill(theirs[n - k - 1], 1 - parity))
            else:
                fill(own[parity], core)
    token_ref[...] = jnp.zeros_like(token_ref)
    out_ref[...] = jnp.dot(block[...], rows[...], preferred_element_type=F32)


def pick_kernel(first_ref, second_ref, out_ref):
    core = lax.axis_index("dp") % 2
    out_ref[0] = first_ref[1 - core]
    out_ref[1] = second_ref[1 - core]


def stack_kernel(*refs):
    for i, ref in enumerate(refs[:-1]):
        refs[-1][i] = ref[...]


def hold_kernel(x_ref, after_ref, out_ref):
    out_ref[...] = x_ref[...]


def half_kernel(plan, partial_ref, mine_ref, after_ref, out_ref):
    n = plan.n_t
    core, t = lax.axis_index("dp") % 2, lax.axis_index("tensor")
    place = jnp.where(core == 0, t, n - 1 - t)
    for j in range(plan.tiles):
        out_ref[j] = partial_ref[t, j].astype(F32) + jnp.where(place >= 1, mine_ref[j].astype(F32), 0.0)


def input_kernel(plan, half_ref, theirs_ref, out_ref):
    n = plan.n_t
    core, t = lax.axis_index("dp") % 2, lax.axis_index("tensor")
    place = jnp.where(core == 0, t, n - 1 - t)
    for j in range(plan.tiles):
        total = half_ref[j] + jnp.where(place < n - 1, theirs_ref[j].astype(F32), 0.0)
        out_ref[:, j * LANES : (j + 1) * LANES] = total.astype(BF16)


def body(mesh, normed, grad_kv, weight):
    plan = Plan(mesh, normed, grad_kv)
    n = plan.n_t
    flat = (plan.tiles, plan.rows, LANES)
    halves = (2, plan.tiles // 2, plan.rows, LANES)
    core = lax.axis_index("dp") % 2

    other_kv = plan.swap_cores(grad_kv)
    near_kv = plan.swap_cores(other_kv) if TWICE else grad_kv
    pieces = pl.pallas_call(
        functools.partial(split_kernel, plan),
        out_shape=[jax.ShapeDtypeStruct((2, plan.rows, plan.window), BF16)] * plan.chips,
        in_specs=[VMEM], out_specs=[VMEM] * plan.chips, compiler_params=PARAMS, name="split",
        cost_estimate=pl.CostEstimate(flops=6 * 10**9, bytes_accessed=0, transcendentals=0),
    )(normed)
    order = range(plan.chips - 1, 0, -1)
    moved = {q: plan.to_chip(pieces[q], q) for q in order}
    pieces = [pieces[0]] + [moved[q] for q in range(1, plan.chips)]

    group = 6
    part_own, part_other = pl.pallas_call(
        functools.partial(partial_kernel, plan),
        out_shape=[jax.ShapeDtypeStruct((n,) + flat, BF16)] * 2,
        grid=(plan.tiles // group,),
        in_specs=[
            pl.BlockSpec(grad_kv.shape, lambda i: (0, 0)),
            pl.BlockSpec(grad_kv.shape, lambda i: (0, 0)),
        ]
        + [pl.BlockSpec((group * LANES // SPLIT, plan.kv), functools.partial(lambda j, i: (SPLIT * i + j, 0), j)) for j in range(SPLIT)],
        out_specs=[pl.BlockSpec((n, group, plan.rows, LANES), lambda i: (0, i, 0, 0))] * 2,
        compiler_params=PARAMS, name="partials",
        cost_estimate=pl.CostEstimate(flops=4 * grad_kv.size * plan.feats, bytes_accessed=weight.size * 2 + 2 * n * normed.size * 2, transcendentals=0),
    )(near_kv, other_kv, *[weight] * SPLIT)

    first = pl.pallas_call(
        functools.partial(turn_kernel, plan),
        out_shape=jax.ShapeDtypeStruct((2, plan.half_tiles, plan.width, LANES), BF16),
        in_specs=[VMEM] * plan.chips + [ANY], out_specs=VMEM,
        scratch_shapes=[pltpu.VMEM((plan.window, LANES), BF16)],
        compiler_params=PARAMS, name="turn",
    )(*pieces, part_own).reshape(flat)
    second = plan.swap_cores(first)

    def passed(received, partial, slot, after):
        return pl.pallas_call(
            functools.partial(pass_kernel, plan, slot),
            out_shape=jax.ShapeDtypeStruct(flat, BF16),
            in_specs=[VMEM] * 2 + [ANY] * len(after), out_specs=VMEM, compiler_params=PARAMS, name="passed",
            cost_estimate=pl.CostEstimate(flops=COST, bytes_accessed=0, transcendentals=0),
        )(received, partial, *after)

    own, theirs = [first.reshape(halves), second.reshape(halves)], []
    first, second = plan.along(first), plan.along(second)

    held_kv = pl.pallas_call(
        hold_kernel, out_shape=jax.ShapeDtypeStruct(grad_kv.shape, BF16),
        in_specs=[VMEM, ANY], out_specs=VMEM, compiler_params=PARAMS, name="hold",
    )(near_kv, part_own)
    kv = pl.pallas_call(
        stack_kernel, out_shape=jax.ShapeDtypeStruct((plan.chips,) + grad_kv.shape, BF16),
        in_specs=[VMEM] * plan.chips, out_specs=VMEM, compiler_params=PARAMS, name="stack",
    )(*[plan.to_chip(held_kv, q) if q else held_kv for q in range(plan.chips)])
    kvs = [kv, plan.swap_cores(kv)]
    trail = [own[1], second]
    for slot in range(2, n + 1):
        got = [first.reshape(halves), second.reshape(halves)]
        own += got
        sent = [passed(first, part_other, slot, [trail[slot - 2]]), passed(second, part_own, slot, theirs[-1:] + ([kvs[1]] if slot == 3 else []))]
        first, second = plan.along(sent[0]), plan.along(sent[1])
        trail.append(second)
        theirs.append(plan.swap_cores(pl.pallas_call(
            pick_kernel, out_shape=jax.ShapeDtypeStruct(halves, BF16), in_specs=[VMEM] * 2, out_specs=VMEM,
            compiler_params=PARAMS, name="pick",
        )(*got)))
    rest = plan.swap_cores(first)

    grad_weight, token = pl.pallas_call(
        functools.partial(weight_kernel, plan),
        out_shape=(jax.ShapeDtypeStruct((plan.width, plan.kv), F32), jax.ShapeDtypeStruct((8, LANES), F32)),
        in_specs=[VMEM] * (3 * n + 1), out_specs=(VMEM, VMEM),
        scratch_shapes=[pltpu.VMEM((plan.width, n * plan.tokens), BF16), pltpu.VMEM((n * plan.tokens, plan.kv), BF16)],
        compiler_params=pltpu.CompilerParams(vmem_limit_bytes=8 * 1024 * 1024 + 4 * n * plan.tokens * (plan.width + plan.kv)), name="weights",
        cost_estimate=pl.CostEstimate(flops=2 * n * normed.size * plan.kv, bytes_accessed=4 * plan.width * plan.kv, transcendentals=0),
    )(*kvs, *own, *theirs)

    half = pl.pallas_call(
        functools.partial(half_kernel, plan),
        out_shape=jax.ShapeDtypeStruct(flat, F32),
        in_specs=[VMEM] * 2 + [ANY], out_specs=VMEM,
        compiler_params=PARAMS, name="half",
        cost_estimate=pl.CostEstimate(flops=COST, bytes_accessed=0, transcendentals=0),
    )(part_own, second, token)
    grad_input = pl.pallas_call(
        functools.partial(input_kernel, plan),
        out_shape=jax.ShapeDtypeStruct(normed.shape, BF16),
        in_specs=[VMEM] * 2, out_specs=VMEM,
        compiler_params=PARAMS, name="inputs",
    )(half, rest)
    return grad_input, grad_weight


def solution(mesh):
    in_specs = (P(("dp", "tensor"), None), P("dp", "tensor"), P(None, "tensor"))
    out_specs = (P(("dp", "tensor"), None), P("dp", "tensor"))
    return jax.shard_map(functools.partial(body, mesh), mesh=mesh, in_specs=in_specs, out_specs=out_specs, check_vma=False)
```

```python
import functools
import math

import jax
import jax.numpy as jnp
from jax import lax
from jax.experimental import pallas as pl
from jax.experimental.pallas import tpu as pltpu
from jax.sharding import PartitionSpec as P

LIMIT = 8
TWICE = 0
SPLIT = 1
ORD = (0, 3, 1, 2)
COST = 4 * 10**8
BF16 = jnp.bfloat16
F32 = jnp.float32
LANES = 128
VMEM = pl.BlockSpec(memory_space=pltpu.VMEM)
ANY = pl.BlockSpec(memory_space=pl.ANY)
PARAMS = pltpu.CompilerParams(vmem_limit_bytes=LIMIT * 1024 * 1024)


class Plan:
    def __init__(self, mesh, normed, grad_kv):
        self.n_dp, self.n_t = mesh.shape["dp"], mesh.shape["tensor"]
        self.chips = self.n_dp // 2
        self.rows, self.feats = normed.shape
        self.kv = grad_kv.shape[1]
        self.width = self.feats // self.n_dp
        self.tokens = self.rows * self.n_dp
        self.tiles = self.feats // LANES
        self.half_tiles = self.tokens // 2 // LANES
        starts = [self.width * d // LANES * LANES for d in range(self.n_dp)]
        ends = [self.width * d - s + self.width for d, s in enumerate(starts)]
        self.window = -(-max(ends) // LANES) * LANES
        self.step = math.gcd(self.width, LANES)
        self.power = self.chips & (self.chips - 1) == 0

    def chip_to(self, chip, q):
        return chip ^ q if self.power else lax.rem(chip + q, self.chips) if not isinstance(chip, int) else (chip + q) % self.chips

    def chip_from(self, chip, q):
        return chip ^ q if self.power else lax.rem(chip + self.chips - q, self.chips)

    def start_of(self, d):
        exact = d * self.width
        return jnp.minimum(exact // LANES * LANES, self.feats - self.window)

    def swap_cores(self, x):
        return lax.ppermute(x, "dp", [(d, d ^ 1) for d in range(self.n_dp)])

    def to_chip(self, x, q):
        return lax.ppermute(x, "dp", [(d, 2 * self.chip_to(d // 2, q) + d % 2) for d in range(self.n_dp)])

    def along(self, x):
        pairs = []
        for d in range(self.n_dp):
            for t in range(self.n_t):
                to = t - 1 if d % 2 else t + 1
                pairs.append((d * self.n_t + t, d * self.n_t + to if 0 <= to < self.n_t else (d ^ 1) * self.n_t + t))
        return lax.ppermute(x, ("dp", "tensor"), pairs)


def split_kernel(plan, normed_ref, *out_refs):
    chip = lax.axis_index("dp") // 2
    for q, out_ref in enumerate(out_refs):
        for group in range(2):
            start = pl.multiple_of(plan.start_of(2 * plan.chip_to(chip, q) + group), LANES)
            out_ref[group] = normed_ref[:, pl.ds(start, plan.window)]


def turn_kernel(plan, *refs):
    pieces, out_ref, scratch = [refs[ORD.index(q)] for q in range(plan.chips)] if plan.chips == 4 else refs[: plan.chips], refs[-2], refs[-1]
    chip = lax.axis_index("dp") // 2
    per_tile = LANES // plan.rows
    for group in range(2):
        d = 2 * chip + group
        offset = pl.multiple_of(d * plan.width - plan.start_of(d), plan.step)
        for j in range(plan.half_tiles):
            tile = jnp.concatenate([ref[group] for ref in pieces[j * per_tile : (j + 1) * per_tile]], axis=0)
            scratch[...] = tile.T
            out_ref[group, j] = scratch[pl.ds(offset, plan.width), :]


def partial_kernel(plan, own_ref, other_ref, *refs):
    weights, out_refs = refs[:-2], refs[-2:]
    both = jnp.concatenate([own_ref[...], other_ref[...]], axis=0)
    product = lax.dot_general(both, jnp.concatenate([ref[...] for ref in weights], axis=0), (((1,), (1,)), ((), ())), preferred_element_type=F32).astype(BF16)
    for half, out_ref in enumerate(out_refs):
        for r in range(plan.n_t):
            at = (half * plan.n_t + r) * plan.rows
            for j in range(out_ref.shape[1]):
                out_ref[r, j] = product[at : at + plan.rows, j * LANES : (j + 1) * LANES]


def pass_kernel(plan, slot, received_ref, partial_ref, *refs):
    n, out_ref = plan.n_t, refs[-1]
    core, t = lax.axis_index("dp") % 2, lax.axis_index("tensor")
    place = jnp.where(core == 0, t, n - 1 - t)
    target = jnp.clip(jnp.where(core == 0, t + n - slot + 1, t - (n - slot + 1)), 0, n - 1)

    @pl.when(place >= slot - 1)
    def _():
        out_ref[...] = received_ref[...]

    @pl.when(place == 0)
    def _():
        out_ref[...] = partial_ref[target]

    @pl.when((place > 0) & (place < slot - 1))
    def _():
        for j in range(plan.tiles):
            out_ref[j] = (received_ref[j].astype(F32) + partial_ref[target, j].astype(F32)).astype(BF16)


def weight_kernel(plan, *refs):
    n, half = plan.n_t, plan.tokens // 2 // plan.n_t
    kv_refs, own, theirs = refs[:2], refs[2 : 2 + 2 * n], refs[2 + 2 * n : -4]
    out_ref, token_ref, block, rows = refs[-4:]
    core, t = lax.axis_index("dp") % 2, lax.axis_index("tensor")
    place = jnp.where(core == 0, t, n - 1 - t)
    shape = (plan.half_tiles, plan.width, LANES)
    for k in range(n):
        source = jnp.where(core == 0, lax.rem(t + n - k, n), lax.rem(t + k, n))
        at = pl.ds(pl.multiple_of(source * plan.rows, plan.rows), plan.rows)
        for parity in range(2):
            begin = (2 * k + parity) * plan.half_tiles * LANES
            for q in range(plan.chips):
                rows[begin + q * plan.rows : begin + (q + 1) * plan.rows, :] = kv_refs[parity][q, at, :]

            def fill(ref, group):
                piece = ref[group].reshape(shape)
                for j in range(plan.half_tiles):
                    block[:, begin + j * LANES : begin + (j + 1) * LANES] = piece[j]

            if k:
                pl.when(place >= k)(lambda: fill(own[2 * k + parity], core))
                pl.when(place < k)(lambda: fill(theirs[n - k - 1], 1 - parity))
            else:
                fill(own[parity], core)
    token_ref[...] = jnp.zeros_like(token_ref)
    out_ref[...] = jnp.dot(block[...], rows[...], preferred_element_type=F32)


def pick_kernel(first_ref, second_ref, out_ref):
    core = lax.axis_index("dp") % 2
    out_ref[0] = first_ref[1 - core]
    out_ref[1] = second_ref[1 - core]


def stack_kernel(count, *refs):
    for i, ref in enumerate(refs[:count]):
        refs[-1][i] = ref[...]


def hold_kernel(x_ref, after_ref, out_ref):
    out_ref[...] = x_ref[...]


def half_kernel(plan, partial_ref, mine_ref, after_ref, out_ref):
    n = plan.n_t
    core, t = lax.axis_index("dp") % 2, lax.axis_index("tensor")
    place = jnp.where(core == 0, t, n - 1 - t)
    for j in range(plan.tiles):
        out_ref[j] = partial_ref[t, j].astype(F32) + jnp.where(place >= 1, mine_ref[j].astype(F32), 0.0)


def input_kernel(plan, half_ref, theirs_ref, out_ref):
    n = plan.n_t
    core, t = lax.axis_index("dp") % 2, lax.axis_index("tensor")
    place = jnp.where(core == 0, t, n - 1 - t)
    for j in range(plan.tiles):
        total = half_ref[j] + jnp.where(place < n - 1, theirs_ref[j].astype(F32), 0.0)
        out_ref[:, j * LANES : (j + 1) * LANES] = total.astype(BF16)


def body(mesh, normed, grad_kv, weight):
    plan = Plan(mesh, normed, grad_kv)
    n = plan.n_t
    flat = (plan.tiles, plan.rows, LANES)
    halves = (2, plan.tiles // 2, plan.rows, LANES)
    core = lax.axis_index("dp") % 2

    other_kv = plan.swap_cores(grad_kv)
    near_kv = plan.swap_cores(other_kv) if TWICE else grad_kv
    pieces = pl.pallas_call(
        functools.partial(split_kernel, plan),
        out_shape=[jax.ShapeDtypeStruct((2, plan.rows, plan.window), BF16)] * plan.chips,
        in_specs=[VMEM], out_specs=[VMEM] * plan.chips, compiler_params=PARAMS, name="split",
        cost_estimate=pl.CostEstimate(flops=6 * 10**9, bytes_accessed=0, transcendentals=0),
    )(normed)
    order = range(plan.chips - 1, 0, -1)
    moved = {q: plan.to_chip(pieces[q], q) for q in order}
    pieces = [pieces[0]] + [moved[q] for q in range(1, plan.chips)]

    group = 6
    part_own, part_other = pl.pallas_call(
        functools.partial(partial_kernel, plan),
        out_shape=[jax.ShapeDtypeStruct((n,) + flat, BF16)] * 2,
        grid=(plan.tiles // group,),
        in_specs=[
            pl.BlockSpec(grad_kv.shape, lambda i: (0, 0)),
            pl.BlockSpec(grad_kv.shape, lambda i: (0, 0)),
        ]
        + [pl.BlockSpec((group * LANES // SPLIT, plan.kv), functools.partial(lambda j, i: (SPLIT * i + j, 0), j)) for j in range(SPLIT)],
        out_specs=[pl.BlockSpec((n, group, plan.rows, LANES), lambda i: (0, i, 0, 0))] * 2,
        compiler_params=PARAMS, name="partials",
        cost_estimate=pl.CostEstimate(flops=4 * grad_kv.size * plan.feats, bytes_accessed=weight.size * 2 + 2 * n * normed.size * 2, transcendentals=0),
    )(near_kv, other_kv, *[weight] * SPLIT)

    first = pl.pallas_call(
        functools.partial(turn_kernel, plan),
        out_shape=jax.ShapeDtypeStruct((2, plan.half_tiles, plan.width, LANES), BF16),
        in_specs=[VMEM] * plan.chips + [ANY], out_specs=VMEM,
        scratch_shapes=[pltpu.VMEM((plan.window, LANES), BF16)],
        compiler_params=PARAMS, name="turn",
    )(*([pieces[q] for q in ORD] if plan.chips == 4 else pieces), part_own).reshape(flat)
    second = plan.swap_cores(first)

    def passed(received, partial, slot, after):
        return pl.pallas_call(
            functools.partial(pass_kernel, plan, slot),
            out_shape=jax.ShapeDtypeStruct(flat, BF16),
            in_specs=[VMEM] * 2 + [ANY] * len(after), out_specs=VMEM, compiler_params=PARAMS, name="passed",
            cost_estimate=pl.CostEstimate(flops=COST, bytes_accessed=0, transcendentals=0),
        )(received, partial, *after)

    own, theirs = [first.reshape(halves), second.reshape(halves)], []
    first, second = plan.along(first), plan.along(second)

    held_kv = pl.pallas_call(
        hold_kernel, out_shape=jax.ShapeDtypeStruct(grad_kv.shape, BF16),
        in_specs=[VMEM, ANY], out_specs=VMEM, compiler_params=PARAMS, name="hold",
    )(near_kv, part_own)
    trail = [own[1], second]
    for slot in range(2, n + 1):
        got = [first.reshape(halves), second.reshape(halves)]
        own += got
        sent = [passed(first, part_other, slot, [trail[slot - 2]]), passed(second, part_own, slot, theirs[-1:] + ([kvs[1]] if slot == 3 else []))]
        first, second = plan.along(sent[0]), plan.along(sent[1])
        if slot == 2:
            kv = pl.pallas_call(
                functools.partial(stack_kernel, plan.chips), out_shape=jax.ShapeDtypeStruct((plan.chips,) + grad_kv.shape, BF16),
                in_specs=[VMEM] * plan.chips + [ANY], out_specs=VMEM, compiler_params=PARAMS, name="stack",
            )(*[plan.to_chip(held_kv, q) if q else held_kv for q in range(plan.chips)], sent[1])
            kvs = [kv, plan.swap_cores(kv)]
        trail.append(second)
        theirs.append(plan.swap_cores(pl.pallas_call(
            pick_kernel, out_shape=jax.ShapeDtypeStruct(halves, BF16), in_specs=[VMEM] * 2, out_specs=VMEM,
            compiler_params=PARAMS, name="pick",
        )(*got)))
    rest = plan.swap_cores(first)

    grad_weight, token = pl.pallas_call(
        functools.partial(weight_kernel, plan),
        out_shape=(jax.ShapeDtypeStruct((plan.width, plan.kv), F32), jax.ShapeDtypeStruct((8, LANES), F32)),
        in_specs=[VMEM] * (3 * n + 1), out_specs=(VMEM, VMEM),
        scratch_shapes=[pltpu.VMEM((plan.width, n * plan.tokens), BF16), pltpu.VMEM((n * plan.tokens, plan.kv), BF16)],
        compiler_params=pltpu.CompilerParams(vmem_limit_bytes=8 * 1024 * 1024 + 4 * n * plan.tokens * (plan.width + plan.kv)), name="weights",
        cost_estimate=pl.CostEstimate(flops=2 * n * normed.size * plan.kv, bytes_accessed=4 * plan.width * plan.kv, transcendentals=0),
    )(*kvs, *own, *theirs)

    half = pl.pallas_call(
        functools.partial(half_kernel, plan),
        out_shape=jax.ShapeDtypeStruct(flat, F32),
        in_specs=[VMEM] * 2 + [ANY], out_specs=VMEM,
        compiler_params=PARAMS, name="half",
        cost_estimate=pl.CostEstimate(flops=COST, bytes_accessed=0, transcendentals=0),
    )(part_own, second, token)
    grad_input = pl.pallas_call(
        functools.partial(input_kernel, plan),
        out_shape=jax.ShapeDtypeStruct(normed.shape, BF16),
        in_specs=[VMEM] * 2, out_specs=VMEM,
        compiler_params=PARAMS, name="inputs",
    )(half, rest)
    return grad_input, grad_weight


def solution(mesh):
    in_specs = (P(("dp", "tensor"), None), P("dp", "tensor"), P(None, "tensor"))
    out_specs = (P(("dp", "tensor"), None), P("dp", "tensor"))
    return jax.shard_map(functools.partial(body, mesh), mesh=mesh, in_specs=in_specs, out_specs=out_specs, check_vma=False)
```

```python
import functools
import math

import jax
import jax.numpy as jnp
from jax import lax
from jax.experimental import pallas as pl
from jax.experimental.pallas import tpu as pltpu
from jax.sharding import PartitionSpec as P

LIMIT = 8
TWICE = 0
SPLIT = 1
ORD = (0, 3, 1, 2)
COST = 4 * 10**8
BF16 = jnp.bfloat16
F32 = jnp.float32
LANES = 128
VMEM = pl.BlockSpec(memory_space=pltpu.VMEM)
ANY = pl.BlockSpec(memory_space=pl.ANY)
PARAMS = pltpu.CompilerParams(vmem_limit_bytes=LIMIT * 1024 * 1024)


class Plan:
    def __init__(self, mesh, normed, grad_kv):
        self.n_dp, self.n_t = mesh.shape["dp"], mesh.shape["tensor"]
        self.chips = self.n_dp // 2
        self.rows, self.feats = normed.shape
        self.kv = grad_kv.shape[1]
        self.width = self.feats // self.n_dp
        self.tokens = self.rows * self.n_dp
        self.tiles = self.feats // LANES
        self.half_tiles = self.tokens // 2 // LANES
        pair = 2 * self.width
        ends = [pair * m % LANES + pair for m in range(self.chips)]
        self.window = -(-max(ends) // LANES) * LANES
        self.step = math.gcd(self.width, LANES)
        self.power = self.chips & (self.chips - 1) == 0

    def chip_to(self, chip, q):
        return chip ^ q if self.power else lax.rem(chip + q, self.chips) if not isinstance(chip, int) else (chip + q) % self.chips

    def chip_from(self, chip, q):
        return chip ^ q if self.power else lax.rem(chip + self.chips - q, self.chips)

    def start_of(self, chip):
        exact = 2 * chip * self.width
        return jnp.minimum(exact // LANES * LANES, self.feats - self.window)

    def swap_cores(self, x):
        return lax.ppermute(x, "dp", [(d, d ^ 1) for d in range(self.n_dp)])

    def to_chip(self, x, q):
        return lax.ppermute(x, "dp", [(d, 2 * self.chip_to(d // 2, q) + d % 2) for d in range(self.n_dp)])

    def along(self, x):
        pairs = []
        for d in range(self.n_dp):
            for t in range(self.n_t):
                to = t - 1 if d % 2 else t + 1
                pairs.append((d * self.n_t + t, d * self.n_t + to if 0 <= to < self.n_t else (d ^ 1) * self.n_t + t))
        return lax.ppermute(x, ("dp", "tensor"), pairs)


def split_kernel(plan, normed_ref, *out_refs):
    chip = lax.axis_index("dp") // 2
    for q, out_ref in enumerate(out_refs):
        start = pl.multiple_of(plan.start_of(plan.chip_to(chip, q)), LANES)
        out_ref[...] = normed_ref[:, pl.ds(start, plan.window)]


def turn_kernel(plan, *refs):
    pieces, out_ref, scratch = [refs[ORD.index(q)] for q in range(plan.chips)] if plan.chips == 4 else refs[: plan.chips], refs[-2], refs[-1]
    chip = lax.axis_index("dp") // 2
    per_tile = LANES // plan.rows
    begin = 2 * chip * plan.width - plan.start_of(chip)
    for j in range(plan.half_tiles):
        tile = jnp.concatenate([ref[...] for ref in pieces[j * per_tile : (j + 1) * per_tile]], axis=0)
        scratch[...] = tile.T
        for group in range(2):
            offset = pl.multiple_of(begin + group * plan.width, plan.step)
            out_ref[group, j] = scratch[pl.ds(offset, plan.width), :]


def partial_kernel(plan, own_ref, other_ref, *refs):
    weights, out_refs = refs[:-2], refs[-2:]
    both = jnp.concatenate([own_ref[...], other_ref[...]], axis=0)
    product = lax.dot_general(both, jnp.concatenate([ref[...] for ref in weights], axis=0), (((1,), (1,)), ((), ())), preferred_element_type=F32).astype(BF16)
    for half, out_ref in enumerate(out_refs):
        for r in range(plan.n_t):
            at = (half * plan.n_t + r) * plan.rows
            for j in range(out_ref.shape[1]):
                out_ref[r, j] = product[at : at + plan.rows, j * LANES : (j + 1) * LANES]


def pass_kernel(plan, slot, received_ref, partial_ref, *refs):
    n, out_ref = plan.n_t, refs[-1]
    core, t = lax.axis_index("dp") % 2, lax.axis_index("tensor")
    place = jnp.where(core == 0, t, n - 1 - t)
    target = jnp.clip(jnp.where(core == 0, t + n - slot + 1, t - (n - slot + 1)), 0, n - 1)

    @pl.when(place >= slot - 1)
    def _():
        out_ref[...] = received_ref[...]

    @pl.when(place == 0)
    def _():
        out_ref[...] = partial_ref[target]

    @pl.when((place > 0) & (place < slot - 1))
    def _():
        for j in range(plan.tiles):
            out_ref[j] = (received_ref[j].astype(F32) + partial_ref[target, j].astype(F32)).astype(BF16)


def weight_kernel(plan, *refs):
    n, half = plan.n_t, plan.tokens // 2 // plan.n_t
    kv_refs, own, theirs = refs[:2], refs[2 : 2 + 2 * n], refs[2 + 2 * n : -4]
    out_ref, token_ref, block, rows = refs[-4:]
    core, t = lax.axis_index("dp") % 2, lax.axis_index("tensor")
    place = jnp.where(core == 0, t, n - 1 - t)
    shape = (plan.half_tiles, plan.width, LANES)
    for k in range(n):
        source = jnp.where(core == 0, lax.rem(t + n - k, n), lax.rem(t + k, n))
        at = pl.ds(pl.multiple_of(source * plan.rows, plan.rows), plan.rows)
        for parity in range(2):
            begin = (2 * k + parity) * plan.half_tiles * LANES
            for q in range(plan.chips):
                rows[begin + q * plan.rows : begin + (q + 1) * plan.rows, :] = kv_refs[parity][q, at, :]

            def fill(ref, group):
                piece = ref[group].reshape(shape)
                for j in range(plan.half_tiles):
                    block[:, begin + j * LANES : begin + (j + 1) * LANES] = piece[j]

            if k:
                pl.when(place >= k)(lambda: fill(own[2 * k + parity], core))
                pl.when(place < k)(lambda: fill(theirs[n - k - 1], 1 - parity))
            else:
                fill(own[parity], core)
    token_ref[...] = jnp.zeros_like(token_ref)
    out_ref[...] = jnp.dot(block[...], rows[...], preferred_element_type=F32)


def pick_kernel(first_ref, second_ref, out_ref):
    core = lax.axis_index("dp") % 2
    out_ref[0] = first_ref[1 - core]
    out_ref[1] = second_ref[1 - core]


def stack_kernel(count, *refs):
    for i, ref in enumerate(refs[:count]):
        refs[-1][i] = ref[...]


def hold_kernel(x_ref, after_ref, out_ref):
    out_ref[...] = x_ref[...]


def half_kernel(plan, partial_ref, mine_ref, after_ref, out_ref):
    n = plan.n_t
    core, t = lax.axis_index("dp") % 2, lax.axis_index("tensor")
    place = jnp.where(core == 0, t, n - 1 - t)
    for j in range(plan.tiles):
        out_ref[j] = partial_ref[t, j].astype(F32) + jnp.where(place >= 1, mine_ref[j].astype(F32), 0.0)


def input_kernel(plan, half_ref, theirs_ref, out_ref):
    n = plan.n_t
    core, t = lax.axis_index("dp") % 2, lax.axis_index("tensor")
    place = jnp.where(core == 0, t, n - 1 - t)
    for j in range(plan.tiles):
        total = half_ref[j] + jnp.where(place < n - 1, theirs_ref[j].astype(F32), 0.0)
        out_ref[:, j * LANES : (j + 1) * LANES] = total.astype(BF16)


def body(mesh, normed, grad_kv, weight):
    plan = Plan(mesh, normed, grad_kv)
    n = plan.n_t
    flat = (plan.tiles, plan.rows, LANES)
    halves = (2, plan.tiles // 2, plan.rows, LANES)
    core = lax.axis_index("dp") % 2

    other_kv = plan.swap_cores(grad_kv)
    near_kv = plan.swap_cores(other_kv) if TWICE else grad_kv
    pieces = pl.pallas_call(
        functools.partial(split_kernel, plan),
        out_shape=[jax.ShapeDtypeStruct((plan.rows, plan.window), BF16)] * plan.chips,
        in_specs=[VMEM], out_specs=[VMEM] * plan.chips, compiler_params=PARAMS, name="split",
        cost_estimate=pl.CostEstimate(flops=6 * 10**9, bytes_accessed=0, transcendentals=0),
    )(normed)
    order = range(plan.chips - 1, 0, -1)
    moved = {q: plan.to_chip(pieces[q], q) for q in order}
    pieces = [pieces[0]] + [moved[q] for q in range(1, plan.chips)]

    group = 6
    part_own, part_other = pl.pallas_call(
        functools.partial(partial_kernel, plan),
        out_shape=[jax.ShapeDtypeStruct((n,) + flat, BF16)] * 2,
        grid=(plan.tiles // group,),
        in_specs=[
            pl.BlockSpec(grad_kv.shape, lambda i: (0, 0)),
            pl.BlockSpec(grad_kv.shape, lambda i: (0, 0)),
        ]
        + [pl.BlockSpec((group * LANES // SPLIT, plan.kv), functools.partial(lambda j, i: (SPLIT * i + j, 0), j)) for j in range(SPLIT)],
        out_specs=[pl.BlockSpec((n, group, plan.rows, LANES), lambda i: (0, i, 0, 0))] * 2,
        compiler_params=PARAMS, name="partials",
        cost_estimate=pl.CostEstimate(flops=4 * grad_kv.size * plan.feats, bytes_accessed=weight.size * 2 + 2 * n * normed.size * 2, transcendentals=0),
    )(near_kv, other_kv, *[weight] * SPLIT)

    first = pl.pallas_call(
        functools.partial(turn_kernel, plan),
        out_shape=jax.ShapeDtypeStruct((2, plan.half_tiles, plan.width, LANES), BF16),
        in_specs=[VMEM] * plan.chips + [ANY], out_specs=VMEM,
        scratch_shapes=[pltpu.VMEM((plan.window, LANES), BF16)],
        compiler_params=PARAMS, name="turn",
    )(*([pieces[q] for q in ORD] if plan.chips == 4 else pieces), part_own).reshape(flat)
    second = plan.swap_cores(first)

    def passed(received, partial, slot, after):
        return pl.pallas_call(
            functools.partial(pass_kernel, plan, slot),
            out_shape=jax.ShapeDtypeStruct(flat, BF16),
            in_specs=[VMEM] * 2 + [ANY] * len(after), out_specs=VMEM, compiler_params=PARAMS, name="passed",
            cost_estimate=pl.CostEstimate(flops=COST, bytes_accessed=0, transcendentals=0),
        )(received, partial, *after)

    own, theirs = [first.reshape(halves), second.reshape(halves)], []
    first, second = plan.along(first), plan.along(second)

    held_kv = pl.pallas_call(
        hold_kernel, out_shape=jax.ShapeDtypeStruct(grad_kv.shape, BF16),
        in_specs=[VMEM, ANY], out_specs=VMEM, compiler_params=PARAMS, name="hold",
    )(near_kv, part_own)
    trail = [own[1], second]
    for slot in range(2, n + 1):
        got = [first.reshape(halves), second.reshape(halves)]
        own += got
        sent = [passed(first, part_other, slot, [trail[slot - 2]]), passed(second, part_own, slot, theirs[-1:] + ([kvs[1]] if slot == 3 else []))]
        first, second = plan.along(sent[0]), plan.along(sent[1])
        if slot == 2:
            kv = pl.pallas_call(
                functools.partial(stack_kernel, plan.chips), out_shape=jax.ShapeDtypeStruct((plan.chips,) + grad_kv.shape, BF16),
                in_specs=[VMEM] * plan.chips + [ANY], out_specs=VMEM, compiler_params=PARAMS, name="stack",
            )(*[plan.to_chip(held_kv, q) if q else held_kv for q in range(plan.chips)], sent[1])
            kvs = [kv, plan.swap_cores(kv)]
        trail.append(second)
        theirs.append(plan.swap_cores(pl.pallas_call(
            pick_kernel, out_shape=jax.ShapeDtypeStruct(halves, BF16), in_specs=[VMEM] * 2, out_specs=VMEM,
            compiler_params=PARAMS, name="pick",
        )(*got)))
    rest = plan.swap_cores(first)

    grad_weight, token = pl.pallas_call(
        functools.partial(weight_kernel, plan),
        out_shape=(jax.ShapeDtypeStruct((plan.width, plan.kv), F32), jax.ShapeDtypeStruct((8, LANES), F32)),
        in_specs=[VMEM] * (3 * n + 1), out_specs=(VMEM, VMEM),
        scratch_shapes=[pltpu.VMEM((plan.width, n * plan.tokens), BF16), pltpu.VMEM((n * plan.tokens, plan.kv), BF16)],
        compiler_params=pltpu.CompilerParams(vmem_limit_bytes=8 * 1024 * 1024 + 4 * n * plan.tokens * (plan.width + plan.kv)), name="weights",
        cost_estimate=pl.CostEstimate(flops=2 * n * normed.size * plan.kv, bytes_accessed=4 * plan.width * plan.kv, transcendentals=0),
    )(*kvs, *own, *theirs)

    half = pl.pallas_call(
        functools.partial(half_kernel, plan),
        out_shape=jax.ShapeDtypeStruct(flat, F32),
        in_specs=[VMEM] * 2 + [ANY], out_specs=VMEM,
        compiler_params=PARAMS, name="half",
        cost_estimate=pl.CostEstimate(flops=COST, bytes_accessed=0, transcendentals=0),
    )(part_own, second, token)
    grad_input = pl.pallas_call(
        functools.partial(input_kernel, plan),
        out_shape=jax.ShapeDtypeStruct(normed.shape, BF16),
        in_specs=[VMEM] * 2, out_specs=VMEM,
        compiler_params=PARAMS, name="inputs",
    )(half, rest)
    return grad_input, grad_weight


def solution(mesh):
    in_specs = (P(("dp", "tensor"), None), P("dp", "tensor"), P(None, "tensor"))
    out_specs = (P(("dp", "tensor"), None), P("dp", "tensor"))
    return jax.shard_map(functools.partial(body, mesh), mesh=mesh, in_specs=in_specs, out_specs=out_specs, check_vma=False)
```

```python
import functools
import math

import jax
import jax.numpy as jnp
from jax import lax
from jax.experimental import pallas as pl
from jax.experimental.pallas import tpu as pltpu
from jax.sharding import PartitionSpec as P

LIMIT = 8
TWICE = 0
SPLIT = 1
ORD = (0, 3, 2, 1)
COST = 4 * 10**8
BF16 = jnp.bfloat16
F32 = jnp.float32
LANES = 128
VMEM = pl.BlockSpec(memory_space=pltpu.VMEM)
ANY = pl.BlockSpec(memory_space=pl.ANY)
PARAMS = pltpu.CompilerParams(vmem_limit_bytes=LIMIT * 1024 * 1024)


class Plan:
    def __init__(self, mesh, normed, grad_kv):
        self.n_dp, self.n_t = mesh.shape["dp"], mesh.shape["tensor"]
        self.chips = self.n_dp // 2
        self.rows, self.feats = normed.shape
        self.kv = grad_kv.shape[1]
        self.width = self.feats // self.n_dp
        self.tokens = self.rows * self.n_dp
        self.tiles = self.feats // LANES
        self.half_tiles = self.tokens // 2 // LANES
        pair = 2 * self.width
        ends = [pair * m % LANES + pair for m in range(self.chips)]
        self.window = -(-max(ends) // LANES) * LANES
        self.step = math.gcd(self.width, LANES)
        self.power = self.chips & (self.chips - 1) == 0

    def chip_to(self, chip, q):
        return chip ^ q if self.power else lax.rem(chip + q, self.chips) if not isinstance(chip, int) else (chip + q) % self.chips

    def chip_from(self, chip, q):
        return chip ^ q if self.power else lax.rem(chip + self.chips - q, self.chips)

    def start_of(self, chip):
        exact = 2 * chip * self.width
        return jnp.minimum(exact // LANES * LANES, self.feats - self.window)

    def swap_cores(self, x):
        return lax.ppermute(x, "dp", [(d, d ^ 1) for d in range(self.n_dp)])

    def to_chip(self, x, q):
        return lax.ppermute(x, "dp", [(d, 2 * self.chip_to(d // 2, q) + d % 2) for d in range(self.n_dp)])

    def along(self, x):
        pairs = []
        for d in range(self.n_dp):
            for t in range(self.n_t):
                to = t - 1 if d % 2 else t + 1
                pairs.append((d * self.n_t + t, d * self.n_t + to if 0 <= to < self.n_t else (d ^ 1) * self.n_t + t))
        return lax.ppermute(x, ("dp", "tensor"), pairs)


def split_kernel(plan, normed_ref, *out_refs):
    chip = lax.axis_index("dp") // 2
    for q, out_ref in enumerate(out_refs):
        start = pl.multiple_of(plan.start_of(plan.chip_to(chip, q)), LANES)
        out_ref[...] = normed_ref[:, pl.ds(start, plan.window)]


def turn_kernel(plan, *refs):
    pieces, out_ref, scratch = [refs[ORD.index(q)] for q in range(plan.chips)] if plan.chips == 4 else refs[: plan.chips], refs[-2], refs[-1]
    chip = lax.axis_index("dp") // 2
    per_tile = LANES // plan.rows
    begin = 2 * chip * plan.width - plan.start_of(chip)
    for j in range(plan.half_tiles):
        tile = jnp.concatenate([ref[...] for ref in pieces[j * per_tile : (j + 1) * per_tile]], axis=0)
        scratch[...] = tile.T
        for group in range(2):
            offset = pl.multiple_of(begin + group * plan.width, plan.step)
            out_ref[group, j] = scratch[pl.ds(offset, plan.width), :]


def partial_kernel(plan, own_ref, other_ref, *refs):
    weights, out_refs = refs[:-2], refs[-2:]
    both = jnp.concatenate([own_ref[...], other_ref[...]], axis=0)
    product = lax.dot_general(both, jnp.concatenate([ref[...] for ref in weights], axis=0), (((1,), (1,)), ((), ())), preferred_element_type=F32).astype(BF16)
    for half, out_ref in enumerate(out_refs):
        for r in range(plan.n_t):
            at = (half * plan.n_t + r) * plan.rows
            for j in range(out_ref.shape[1]):
                out_ref[r, j] = product[at : at + plan.rows, j * LANES : (j + 1) * LANES]


def pass_kernel(plan, slot, received_ref, partial_ref, *refs):
    n, out_ref = plan.n_t, refs[-1]
    core, t = lax.axis_index("dp") % 2, lax.axis_index("tensor")
    place = jnp.where(core == 0, t, n - 1 - t)
    target = jnp.clip(jnp.where(core == 0, t + n - slot + 1, t - (n - slot + 1)), 0, n - 1)

    @pl.when(place >= slot - 1)
    def _():
        out_ref[...] = received_ref[...]

    @pl.when(place == 0)
    def _():
        out_ref[...] = partial_ref[target]

    @pl.when((place > 0) & (place < slot - 1))
    def _():
        for j in range(plan.tiles):
            out_ref[j] = (received_ref[j].astype(F32) + partial_ref[target, j].astype(F32)).astype(BF16)


def weight_kernel(plan, *refs):
    n, half = plan.n_t, plan.tokens // 2 // plan.n_t
    kv_refs, own, theirs = refs[:2], refs[2 : 2 + 2 * n], refs[2 + 2 * n : -4]
    out_ref, token_ref, block, rows = refs[-4:]
    core, t = lax.axis_index("dp") % 2, lax.axis_index("tensor")
    place = jnp.where(core == 0, t, n - 1 - t)
    shape = (plan.half_tiles, plan.width, LANES)
    for k in range(n):
        source = jnp.where(core == 0, lax.rem(t + n - k, n), lax.rem(t + k, n))
        at = pl.ds(pl.multiple_of(source * plan.rows, plan.rows), plan.rows)
        for parity in range(2):
            begin = (2 * k + parity) * plan.half_tiles * LANES
            for q in range(plan.chips):
                rows[begin + q * plan.rows : begin + (q + 1) * plan.rows, :] = kv_refs[parity][q, at, :]

            def fill(ref, group):
                piece = ref[group].reshape(shape)
                for j in range(plan.half_tiles):
                    block[:, begin + j * LANES : begin + (j + 1) * LANES] = piece[j]

            if k:
                pl.when(place >= k)(lambda: fill(own[2 * k + parity], core))
                pl.when(place < k)(lambda: fill(theirs[n - k - 1], 1 - parity))
            else:
                fill(own[parity], core)
    token_ref[...] = jnp.zeros_like(token_ref)
    out_ref[...] = jnp.dot(block[...], rows[...], preferred_element_type=F32)


def pick_kernel(first_ref, second_ref, out_ref):
    core = lax.axis_index("dp") % 2
    out_ref[0] = first_ref[1 - core]
    out_ref[1] = second_ref[1 - core]


def stack_kernel(count, *refs):
    for i, ref in enumerate(refs[:count]):
        refs[-1][i] = ref[...]


def hold_kernel(x_ref, after_ref, out_ref):
    out_ref[...] = x_ref[...]


def half_kernel(plan, partial_ref, mine_ref, after_ref, out_ref):
    n = plan.n_t
    core, t = lax.axis_index("dp") % 2, lax.axis_index("tensor")
    place = jnp.where(core == 0, t, n - 1 - t)
    for j in range(plan.tiles):
        out_ref[j] = partial_ref[t, j].astype(F32) + jnp.where(place >= 1, mine_ref[j].astype(F32), 0.0)


def input_kernel(plan, half_ref, theirs_ref, out_ref):
    n = plan.n_t
    core, t = lax.axis_index("dp") % 2, lax.axis_index("tensor")
    place = jnp.where(core == 0, t, n - 1 - t)
    for j in range(plan.tiles):
        total = half_ref[j] + jnp.where(place < n - 1, theirs_ref[j].astype(F32), 0.0)
        out_ref[:, j * LANES : (j + 1) * LANES] = total.astype(BF16)


def body(mesh, normed, grad_kv, weight):
    plan = Plan(mesh, normed, grad_kv)
    n = plan.n_t
    flat = (plan.tiles, plan.rows, LANES)
    halves = (2, plan.tiles // 2, plan.rows, LANES)
    core = lax.axis_index("dp") % 2

    other_kv = plan.swap_cores(grad_kv)
    near_kv = plan.swap_cores(other_kv) if TWICE else grad_kv
    pieces = pl.pallas_call(
        functools.partial(split_kernel, plan),
        out_shape=[jax.ShapeDtypeStruct((plan.rows, plan.window), BF16)] * plan.chips,
        in_specs=[VMEM], out_specs=[VMEM] * plan.chips, compiler_params=PARAMS, name="split",
        cost_estimate=pl.CostEstimate(flops=6 * 10**9, bytes_accessed=0, transcendentals=0),
    )(normed)
    order = range(plan.chips - 1, 0, -1)
    moved = {q: plan.to_chip(pieces[q], q) for q in order}
    pieces = [pieces[0]] + [moved[q] for q in range(1, plan.chips)]

    group = 6
    part_own, part_other = pl.pallas_call(
        functools.partial(partial_kernel, plan),
        out_shape=[jax.ShapeDtypeStruct((n,) + flat, BF16)] * 2,
        grid=(plan.tiles // group,),
        in_specs=[
            pl.BlockSpec(grad_kv.shape, lambda i: (0, 0)),
            pl.BlockSpec(grad_kv.shape, lambda i: (0, 0)),
        ]
        + [pl.BlockSpec((group * LANES // SPLIT, plan.kv), functools.partial(lambda j, i: (SPLIT * i + j, 0), j)) for j in range(SPLIT)],
        out_specs=[pl.BlockSpec((n, group, plan.rows, LANES), lambda i: (0, i, 0, 0))] * 2,
        compiler_params=PARAMS, name="partials",
        cost_estimate=pl.CostEstimate(flops=4 * grad_kv.size * plan.feats, bytes_accessed=weight.size * 2 + 2 * n * normed.size * 2, transcendentals=0),
    )(near_kv, other_kv, *[weight] * SPLIT)

    first = pl.pallas_call(
        functools.partial(turn_kernel, plan),
        out_shape=jax.ShapeDtypeStruct((2, plan.half_tiles, plan.width, LANES), BF16),
        in_specs=[VMEM] * plan.chips + [ANY], out_specs=VMEM,
        scratch_shapes=[pltpu.VMEM((plan.window, LANES), BF16)],
        compiler_params=PARAMS, name="turn", cost_estimate=pl.CostEstimate(flops=2000000000, bytes_accessed=0, transcendentals=0),
    )(*([pieces[q] for q in ORD] if plan.chips == 4 else pieces), part_own).reshape(flat)
    second = plan.swap_cores(first)

    def passed(received, partial, slot, after):
        return pl.pallas_call(
            functools.partial(pass_kernel, plan, slot),
            out_shape=jax.ShapeDtypeStruct(flat, BF16),
            in_specs=[VMEM] * 2 + [ANY] * len(after), out_specs=VMEM, compiler_params=PARAMS, name="passed",
            cost_estimate=pl.CostEstimate(flops=COST, bytes_accessed=0, transcendentals=0),
        )(received, partial, *after)

    own, theirs = [first.reshape(halves), second.reshape(halves)], []
    first, second = plan.along(first), plan.along(second)

    held_kv = pl.pallas_call(
        hold_kernel, out_shape=jax.ShapeDtypeStruct(grad_kv.shape, BF16),
        in_specs=[VMEM, ANY], out_specs=VMEM, compiler_params=PARAMS, name="hold",
    )(near_kv, own[1])
    trail = [own[1], second]
    for slot in range(2, n + 1):
        got = [first.reshape(halves), second.reshape(halves)]
        own += got
        sent = [passed(first, part_other, slot, []), passed(second, part_own, slot, theirs[-1:] + ([kvs[1]] if slot == 3 else []))]
        first, second = plan.along(sent[0]), plan.along(sent[1])
        if slot == 2:
            kv = pl.pallas_call(
                functools.partial(stack_kernel, plan.chips), out_shape=jax.ShapeDtypeStruct((plan.chips,) + grad_kv.shape, BF16),
                in_specs=[VMEM] * plan.chips + [ANY], out_specs=VMEM, compiler_params=PARAMS, name="stack",
            )(*[plan.to_chip(held_kv, q) if q else held_kv for q in range(plan.chips)], sent[0])
            kvs = [kv, plan.swap_cores(kv)]
        trail.append(second)
        theirs.append(plan.swap_cores(pl.pallas_call(
            pick_kernel, out_shape=jax.ShapeDtypeStruct(halves, BF16), in_specs=[VMEM] * 2, out_specs=VMEM,
            compiler_params=PARAMS, name="pick", cost_estimate=pl.CostEstimate(flops=1000000000, bytes_accessed=0, transcendentals=0),
        )(*got)))
    rest = plan.swap_cores(first)

    grad_weight, token = pl.pallas_call(
        functools.partial(weight_kernel, plan),
        out_shape=(jax.ShapeDtypeStruct((plan.width, plan.kv), F32), jax.ShapeDtypeStruct((8, LANES), F32)),
        in_specs=[VMEM] * (3 * n + 1), out_specs=(VMEM, VMEM),
        scratch_shapes=[pltpu.VMEM((plan.width, n * plan.tokens), BF16), pltpu.VMEM((n * plan.tokens, plan.kv), BF16)],
        compiler_params=pltpu.CompilerParams(vmem_limit_bytes=8 * 1024 * 1024 + 4 * n * plan.tokens * (plan.width + plan.kv)), name="weights",
        cost_estimate=pl.CostEstimate(flops=2 * n * normed.size * plan.kv, bytes_accessed=4 * plan.width * plan.kv, transcendentals=0),
    )(*kvs, *own, *theirs)

    half = pl.pallas_call(
        functools.partial(half_kernel, plan),
        out_shape=jax.ShapeDtypeStruct(flat, F32),
        in_specs=[VMEM] * 2 + [ANY], out_specs=VMEM,
        compiler_params=PARAMS, name="half",
        cost_estimate=pl.CostEstimate(flops=COST, bytes_accessed=0, transcendentals=0),
    )(part_own, second, token)
    grad_input = pl.pallas_call(
        functools.partial(input_kernel, plan),
        out_shape=jax.ShapeDtypeStruct(normed.shape, BF16),
        in_specs=[VMEM] * 2, out_specs=VMEM,
        compiler_params=PARAMS, name="inputs",
    )(half, rest)
    return grad_input, grad_weight


def solution(mesh):
    in_specs = (P(("dp", "tensor"), None), P("dp", "tensor"), P(None, "tensor"))
    out_specs = (P(("dp", "tensor"), None), P("dp", "tensor"))
    return jax.shard_map(functools.partial(body, mesh), mesh=mesh, in_specs=in_specs, out_specs=out_specs, check_vma=False)
```
